128 devices in a mesh: blk: 128 (over z, x, y, core).
Axes of the slice: x: 4, y: 4, z: 4, core: 2. Of those that a mesh axis runs over, the one named last changes fastest.
Arguments:
- features: bfloat16 [256, 65536], P(None, 'blk'), may hold values from -0.8984375 to 0.8984375
- direction: float32 [64, 65536], P(None, 'blk'), may hold values from -240 to 240
- residual: float32 [64, 65536], P(None, 'blk'), may hold values from -240 to 240
- noise_var: float32 [1], replicated, may hold values from 0.3 to 3
Outputs:
- updated_residual_rows: float32 [64, 65536], P(None, 'blk')
- updated_search_direction: float32 [64, 65536], P(None, 'blk')
The draws below stay inside these ranges and needn't reach their ends.
All inputs are finite; a program needn't handle non-finite values.
Results may differ from the reference program's by a relative error of at most 0.0036.
Values may be sent and summed in bfloat16 or wider, within the bound.
A program may use at most 128 MiB of HBM per device.

```python
import math
import jax
import jax.numpy as jnp
from jax import lax

FEAT = 256
COLS = 64
PTS_DEV = 512
POINTS = 65536


def apply_scales(base, row_key, col_key, rise):
    position = jnp.arange(POINTS, dtype=jnp.float32) / (POINTS - 1)
    row_scale = rise ** position * 10.0 ** (jax.random.uniform(row_key, (POINTS,), jnp.float32) - 0.5)
    col_scale = 2.0 ** (2.0 * jax.random.uniform(col_key, (COLS, 1), jnp.float32) - 1.0)
    return base * row_scale[None, :] * col_scale


def draw_residual(key, part):
    key = jax.random.fold_in(key, 11)
    base_key, row_key, col_key = jax.random.split(key, 3)
    base = jax.random.truncated_normal(base_key, -4.0, 4.0, (COLS, POINTS), jnp.float32)
    rise = 3.0
    return apply_scales(base, row_key, col_key, rise)


def draw_direction(key, part):
    key = jax.random.fold_in(key, 23)
    base_key, row_key, col_key = jax.random.split(key, 3)
    base = jax.random.truncated_normal(base_key, -4.0, 4.0, (COLS, POINTS), jnp.float32)
    rise = 3.0
    return apply_scales(base, row_key, col_key, rise)


def block_scale(key, extent, pieces, least, largest):
    factor_of = 1.0
    for axis_at, blocks in pieces:
        draws = jax.random.uniform(jax.random.fold_in(jax.random.fold_in(key, 6), axis_at), (blocks,), jnp.float32, least / len(pieces), largest / len(pieces))
        factor_of = factor_of * jnp.repeat(jnp.exp(draws), extent[axis_at] // blocks).reshape((-1,) + (1,) * (len(extent) - 1 - axis_at))
    return factor_of


def gaussian(rng, shape, deviation, bound, pieces=(), kind=jnp.bfloat16):
    drawn = deviation * jax.random.normal(rng, shape, jnp.float32)
    if pieces:
        drawn = drawn * block_scale(rng, shape, pieces, -0.22, 0.18)
    return jnp.clip(drawn, -bound, bound).astype(kind)


def setup_inputs(seed: int = 0) -> dict:
    key_list = jax.random.split(jax.random.key(seed), 5)
    features = gaussian(key_list[0], (FEAT, POINTS), 0.15, 0.8984375, ((1, 128),))
    direction = draw_direction(jax.random.fold_in(key_list[4], 71), 0)
    residual = draw_residual(jax.random.fold_in(key_list[4], 71), 0)
    noise_var = jnp.clip(jnp.exp(jax.random.uniform(key_list[3], (1,), jnp.float32, math.log(0.3), math.log(3.0))), 0.3, 3.0)
    return dict(features=features, direction=direction, residual=residual, noise_var=noise_var)


def kernel_rows(row_feats, col_feats):
    row_norm = jnp.sum(row_feats * row_feats, axis=0)
    col_norm = jnp.sum(col_feats * col_feats, axis=0)
    gram = jnp.dot(row_feats.T, col_feats, precision=lax.Precision.HIGHEST)
    dist = row_norm[:, None] + col_norm[None, :] - 2.0 * gram
    return jnp.exp(-0.5 * dist).astype(jnp.bfloat16)


def reference(features, direction, residual, noise_var):
    feats_wide = features.astype(jnp.float32)
    dir_half = lax.optimization_barrier(direction.astype(jnp.bfloat16)).astype(jnp.float32)
    count = POINTS // PTS_DEV
    blocks = jnp.moveaxis(feats_wide.reshape(FEAT, count, PTS_DEV), 1, 0)

    def one_block(block_feats):
        tile = lax.optimization_barrier(kernel_rows(block_feats, feats_wide)).astype(jnp.float32)
        return jnp.dot(dir_half, tile.T, precision=lax.Precision.HIGHEST)

    parts = lax.map(one_block, blocks)
    kernel_part = jnp.moveaxis(parts, 0, 1).reshape(COLS, POINTS)
    image = kernel_part + noise_var[0] * direction
    residual_square_sum = jnp.sum(residual * residual, axis=1) + 1e-6
    direction_curvature = jnp.sum(direction * image, axis=1)
    step_length = residual_square_sum / direction_curvature
    updated_residual_rows = residual - step_length[:, None] * image
    updated_residual_square_sum = jnp.sum(updated_residual_rows * updated_residual_rows, axis=1)
    updated_search_direction = updated_residual_rows + (updated_residual_square_sum / residual_square_sum)[:, None] * direction
    return updated_residual_rows, updated_search_direction
```

```python
import functools

import jax
import jax.numpy as jnp
from jax import lax
from jax.experimental import pallas as pl
from jax.experimental.pallas import tpu as pltpu
from jax.sharding import PartitionSpec as P

LOG2E = 1.4426950408889634
MESH = pl.DeviceIdType.MESH
HALF = 256
DIRS = 64
ROWS = HALF + DIRS
GROUP = 4
NGROUP = 8
NEAR = 24

ORDER = (
    ("A", 0, 0), ("B", 0, 0), ("A", 1, 0), ("B", 0, 1),
    ("A", 3, 0), ("B", 0, 3), ("B", 1, 0), ("A", 0, 1),
    ("B", 3, 0), ("A", 0, 3), ("A", 2, 0), ("B", 0, 2),
    ("A", 1, 1), ("A", 1, 3), ("B", 1, 1), ("B", 3, 1),
    ("A", 3, 1), ("A", 3, 3), ("B", 1, 3), ("B", 3, 3),
    ("B", 2, 0), ("A", 0, 2), ("A", 2, 1), ("B", 1, 2),
    ("A", 2, 3), ("B", 3, 2), ("A", 1, 2), ("B", 2, 1),
    ("A", 3, 2), ("B", 2, 3), ("A", 2, 2), ("B", 2, 2),
)
SLOT = {key: at for at, key in enumerate(ORDER)}


def both(half, oz, ox, axis):
    return [(half, oz, ox, axis, -1, None), (half, oz, ox, axis, 1, None)]


def onward(half, other, axis):
    ends = ((1, other), (3, other)) if axis == "z" else ((other, 1), (other, 3))
    return [(half, *ends[0], axis, -1, 0), (half, *ends[1], axis, 1, 1)]


ROUNDS = {
    "1": both("A", 0, 0, "z") + both("B", 0, 0, "x"),
    "2": both("B", 0, 0, "z") + both("A", 0, 0, "x"),
    "3": onward("A", 0, "z") + onward("B", 0, "x"),
    "4a": both("A", 1, 0, "x") + both("B", 0, 1, "z"),
    "4b": both("A", 3, 0, "x") + both("B", 0, 3, "z"),
    "4": onward("B", 0, "z") + onward("A", 0, "x"),
    "5": both("A", 2, 0, "x") + both("B", 0, 2, "z"),
    "6a": onward("A", 1, "x") + onward("B", 1, "z"),
    "6b": onward("A", 3, "x") + onward("B", 3, "z"),
    "7": onward("A", 2, "x") + onward("B", 2, "z"),
}
FIRST = {}
for _name, _moves in ROUNDS.items():
    FIRST[_name] = sum(len(ROUNDS[n]) for n in FIRST)
N_Q = sum(len(m) for m in ROUNDS.values())
DY = (0, 1, 3, 2)


def kernel(feat, direction, residual, noise, new_res, new_dir,
           xq, xp, acc, hq, hp, back, mine, one, two,
           q_send, q_recv, p_send, p_recv, b_send, b_recv, s_send, s_recv):
    me = lax.axis_index("blk")
    core = lax.rem(me, 2)
    y = lax.rem(me // 2, 4)
    x = lax.rem(me // 8, 4)
    z = me // 32

    def dev(dz, dx, dy, dc):
        nz, nx, ny = lax.rem(z + dz, 4), lax.rem(x + dx, 4), lax.rem(y + dy, 4)
        nc = 1 - core if dc else core
        return (((nz * 4 + nx) * 4 + ny) * 2 + nc,)

    def remote(src, dst, send, recv, to):
        return pltpu.make_async_remote_copy(
            src_ref=src, dst_ref=dst, send_sem=send, recv_sem=recv, device_id=to, device_id_type=MESH
        )

    def q_copies(name):
        out = []
        for at, (half, oz, ox, axis, sign, piece) in enumerate(ROUNDS[name]):
            dz, dx = (sign, 0) if axis == "z" else (0, sign)
            src = xq.at[SLOT[half, oz, ox]]
            dst = xq.at[SLOT[half, (oz - dz) % 4, (ox - dx) % 4]]
            if piece is not None:
                rows = pl.ds(piece * (ROWS // 2), ROWS // 2)
                src, dst = src.at[rows], dst.at[rows]
            k = FIRST[name] + at
            out.append(remote(src, dst, q_send.at[k], q_recv.at[k], dev(dz % 4, dx % 4, 0, 0)))
        return out

    def p_copy(k):
        low, high = pl.ds(0, 128), pl.ds(128, 128)
        src, dst, to = (
            lambda: (feat, xp.at[core], dev(0, 0, 0, 1)),
            lambda: (feat, xp.at[2 + core], dev(0, 0, 3, 0)),
            lambda: (feat, xp.at[4 + core], dev(0, 0, 1, 0)),
            lambda: (xp.at[2 + core], xp.at[2 + core], dev(0, 0, 0, 1)),
            lambda: (xp.at[4 + core], xp.at[4 + core], dev(0, 0, 0, 1)),
            lambda: (xp.at[2 + core, low], xp.at[6 + core, low], dev(0, 0, 3, 0)),
            lambda: (xp.at[4 + core, high], xp.at[6 + core, high], dev(0, 0, 1, 0)),
            lambda: (xp.at[6 + core], xp.at[6 + core], dev(0, 0, 0, 1)),
        )[k]()
        return remote(src, dst, p_send.at[k], p_recv.at[k], to)

    def back_copy(j, dc):
        target = 1 - core if dc else core
        k = DY[j] * 2 + dc - 1
        return remote(acc.at[2 * j + target], back.at[k], b_send.at[k], b_recv.at[k], dev(0, 0, DY[j], dc))

    def start(copies):
        for copy in copies:
            copy.start()

    def arrived(copies):
        for copy in copies:
            copy.wait_recv()

    group = [(dy, dc) for dy in range(4) for dc in range(2)][1:]
    plane = [(dz, dx) for dz in range(4) for dx in range(4)][1:]

    barrier = pltpu.get_barrier_semaphore()
    for dy, dc in group:
        pl.semaphore_signal(barrier, inc=1, device_id=dev(0, 0, dy, dc), device_id_type=MESH)
    for dz, dx in plane:
        pl.semaphore_signal(barrier, inc=1, device_id=dev(dz, dx, 0, 0), device_id_type=MESH)

    for at in range(2):
        cols = pl.ds(at * HALF, HALF)
        xq[at, 0:HALF, :] = feat[:, cols].T
        xq[at, HALF:ROWS, :] = direction[:, cols].astype(jnp.bfloat16)
    xp[core] = feat[...]
    acc[...] = jnp.zeros_like(acc)

    pl.semaphore_wait(barrier, len(group) + len(plane))
    start(q_copies("1"))
    start([p_copy(0), p_copy(1), p_copy(2)])

    def task(t, carry):
        far = t - NEAR
        turn = far // 2
        late = t >= NEAR
        g = jnp.where(late, NGROUP - 2 + lax.rem(jnp.maximum(far, 0), 2), t // GROUP)
        last_j = jnp.where(turn == 0, 3, jnp.where(turn == 3, 0, turn))
        j = jnp.where(late, last_j, lax.rem(t, GROUP))

        @pl.when(t == 0)
        def _():
            arrived(q_copies("1"))
            start(q_copies("2"))
            start(q_copies("3"))
            arrived([p_copy(0)])

        @pl.when(t == 1)
        def _():
            arrived([p_copy(1), p_copy(2)])
            start([p_copy(3), p_copy(4), p_copy(5), p_copy(6)])
            arrived([p_copy(3)])

        @pl.when(t == 2)
        def _():
            start(q_copies("4a"))
            arrived([p_copy(4)])

        @pl.when(t == 3)
        def _():
            arrived([p_copy(5), p_copy(6)])
            start([p_copy(7)])
            arrived([p_copy(7)])

        @pl.when(t == 4)
        def _():
            arrived(q_copies("2"))
            start(q_copies("4b"))

        @pl.when(t == 6)
        def _():
            arrived(q_copies("3"))
            start(q_copies("4"))

        @pl.when(t == 8)
        def _():
            start(q_copies("5"))

        @pl.when(t == 12)
        def _():
            arrived(q_copies("4a"))
            start(q_copies("6a"))

        @pl.when(t == 14)
        def _():
            arrived(q_copies("4b"))
            start(q_copies("6b"))

        @pl.when(t == 18)
        def _():
            arrived(q_copies("5"))
            start(q_copies("7"))

        @pl.when(t == 20)
        def _():
            arrived(q_copies("4"))

        @pl.when(t == NEAR)
        def _():
            arrived(q_copies("6a"))
            arrived(q_copies("6b"))

        @pl.when(t == NEAR + 1)
        def _():
            arrived(q_copies("7"))

        for after, chunk in ((NEAR + 2, 3), (NEAR + 4, 1), (NEAR + 6, 2)):
            @pl.when(t == after)
            def _(chunk=chunk):
                start([back_copy(chunk, 0), back_copy(chunk, 1)])

        slots = pl.ds(g * GROUP, GROUP)
        points = pl.ds(pl.multiple_of(g * GROUP * HALF, GROUP * HALF), GROUP * HALF)

        @pl.when(t < 4)
        def _():
            for c in range(2):
                wide = xp[2 * j + c].astype(jnp.float32)
                hp[j, :, c * 512:(c + 1) * 512] = (0.5 * LOG2E) * jnp.sum(wide * wide, axis=0, keepdims=True)

        @pl.when(jnp.logical_or(j == 0, jnp.logical_and(late, turn == 0)))
        def _():
            wide = xq[slots, 0:HALF, :].reshape(GROUP * HALF, HALF).astype(jnp.float32)
            hq[points, :] = (0.5 * LOG2E) * jnp.sum(wide * wide, axis=1, keepdims=True)

        rows = xq[slots, 0:HALF, :].reshape(GROUP * HALF, HALF)
        cols = jnp.concatenate([xp[2 * j], xp[2 * j + 1]], axis=1)
        gram = jnp.dot(rows, cols, preferred_element_type=jnp.float32)
        tile = jnp.exp2(gram * LOG2E - hq[points, :] - hp[j]).astype(jnp.bfloat16)
        dirs = jnp.concatenate([xq[g * GROUP + i, HALF:ROWS, :] for i in range(GROUP)], axis=1)
        part = jnp.dot(dirs, tile, preferred_element_type=jnp.float32)
        acc[2 * j] += part[:, :512]
        acc[2 * j + 1] += part[:, 512:]
        return carry

    lax.fori_loop(0, NGROUP * GROUP, task, 0)

    start([back_copy(0, 1)])
    backs = [back_copy(j, dc) for j in (3, 1, 2, 0) for dc in range(2) if (j, dc) != (0, 0)]
    total = acc[core] + noise[0] * direction[...]
    for copy in backs:
        copy.wait_recv()
    for k in range(7):
        total = total + back[k]
    acc[core] = total
    res, way = residual[...], direction[...]
    sums = [jnp.sum(v, axis=1, keepdims=True) for v in (res * res, way * total, res * total, total * total)]
    lane = lax.broadcasted_iota(jnp.int32, (DIRS, 128), 1)
    packed = jnp.zeros((DIRS, 128), jnp.float32)
    for k, v in enumerate(sums):
        packed = jnp.where(lane == k, v, packed)
    packed = jnp.concatenate([packed, jnp.zeros((128 - DIRS, 128), jnp.float32)], axis=0).T
    mine[0] = packed[0:8]

    firsts = [remote(mine.at[0], one.at[k], s_send.at[k], s_recv.at[k], dev(0, 0, dy, dc))
              for k, (dy, dc) in enumerate(group)]
    start(firsts)
    arrived(firsts)
    so_far = mine[0]
    for k in range(len(group)):
        so_far = so_far + one[k]
    mine[1] = so_far
    n = len(group)
    seconds = [remote(mine.at[1], two.at[k], s_send.at[n + k], s_recv.at[n + k], dev(dz, dx, 0, 0))
               for k, (dz, dx) in enumerate(plane)]
    start(seconds)
    arrived(seconds)
    for k in range(len(plane)):
        so_far = so_far + two[k]
    columns = jnp.concatenate([so_far, jnp.zeros((120, 128), jnp.float32)], axis=0).T
    rr, curv, ri, ii = [columns[0:DIRS, k:k + 1] for k in range(4)]
    rsq = rr + 1e-6
    alpha = rsq / curv
    fresh = residual[...] - alpha * acc[core]
    new_res[...] = fresh
    rsq_next = rr - alpha * (2.0 * ri - alpha * ii)
    new_dir[...] = fresh + (rsq_next / rsq) * direction[...]

    for name in ROUNDS:
        for copy in q_copies(name):
            copy.wait_send()
    for k in range(8):
        p_copy(k).wait_send()
    for copy in backs + firsts + seconds:
        copy.wait_send()


def shards(features, direction, residual, noise_var):
    vmem = pl.BlockSpec(memory_space=pltpu.VMEM)
    shape = jax.ShapeDtypeStruct(direction.shape, jnp.float32)
    points = direction.shape[1]
    dma = pltpu.SemaphoreType.DMA
    return pl.pallas_call(
        kernel,
        out_shape=(shape, shape),
        in_specs=[vmem, vmem, vmem, pl.BlockSpec(memory_space=pltpu.SMEM)],
        out_specs=(vmem, vmem),
        scratch_shapes=[
            pltpu.VMEM((NGROUP * GROUP, ROWS, HALF), jnp.bfloat16),
            pltpu.VMEM((8, 256, points), jnp.bfloat16),
            pltpu.VMEM((8, DIRS, points), jnp.float32),
            pltpu.VMEM((NGROUP * GROUP * HALF, 1), jnp.float32),
            pltpu.VMEM((4, 1, 2 * points), jnp.float32),
            pltpu.VMEM((7, DIRS, points), jnp.float32),
            pltpu.VMEM((2, 8, 128), jnp.float32),
            pltpu.VMEM((7, 8, 128), jnp.float32),
            pltpu.VMEM((15, 8, 128), jnp.float32),
            dma((N_Q,)), dma((N_Q,)), dma((8,)), dma((8,)), dma((7,)), dma((7,)), dma((22,)), dma((22,)),
        ],
        compiler_params=pltpu.CompilerParams(
            collective_id=0, has_side_effects=True, vmem_limit_bytes=56 * 2**20
        ),
    )(features, direction, residual, noise_var)


def solution(mesh):
    return jax.shard_map(
        shards,
        mesh=mesh,
        in_specs=(P(None, "blk"), P(None, "blk"), P(None, "blk"), P()),
        out_specs=(P(None, "blk"), P(None, "blk")),
        check_vma=False,
    )
```

```python
import jax
import jax.numpy as jnp
from jax import lax
from jax.experimental import pallas as pl
from jax.experimental.pallas import tpu as pltpu
from jax.sharding import PartitionSpec as P

LOG2E = 1.4426950408889634
MESH = pl.DeviceIdType.MESH
HALF = 256
DIRS = 64
ROWS = HALF + DIRS
GROUP = 4
NGROUP = 8
LATE = 5
NEAR = LATE * GROUP
FAR = NGROUP - LATE

ORDER = (
    ("A", 0, 0), ("B", 0, 0), ("A", 1, 0), ("B", 0, 1),
    ("A", 3, 0), ("B", 0, 3), ("B", 1, 0), ("A", 0, 1),
    ("B", 3, 0), ("A", 0, 3), ("A", 2, 0), ("B", 0, 2),
    ("A", 1, 1), ("A", 1, 3), ("B", 1, 1), ("B", 3, 1),
    ("A", 3, 1), ("A", 3, 3), ("B", 1, 3), ("B", 3, 3),
    ("B", 2, 0), ("A", 0, 2), ("A", 2, 1), ("B", 1, 2),
    ("A", 2, 3), ("B", 3, 2), ("A", 1, 2), ("B", 2, 1),
    ("A", 3, 2), ("B", 2, 3), ("A", 2, 2), ("B", 2, 2),
)
SLOT = {key: at for at, key in enumerate(ORDER)}


def both(half, oz, ox, axis):
    return [(half, oz, ox, axis, -1, None), (half, oz, ox, axis, 1, None)]


def onward(half, other, axis):
    ends = ((1, other), (3, other)) if axis == "z" else ((other, 1), (other, 3))
    return [(half, *ends[0], axis, -1, 0), (half, *ends[1], axis, 1, 1)]


ROUNDS = {
    "1": both("A", 0, 0, "z") + both("B", 0, 0, "x"),
    "2": both("B", 0, 0, "z") + both("A", 0, 0, "x"),
    "3": onward("A", 0, "z") + onward("B", 0, "x"),
    "4a": both("A", 1, 0, "x") + both("B", 0, 1, "z"),
    "4b": both("A", 3, 0, "x") + both("B", 0, 3, "z"),
    "4": onward("B", 0, "z") + onward("A", 0, "x"),
    "5": both("A", 2, 0, "x") + both("B", 0, 2, "z"),
    "6a": onward("A", 1, "x") + onward("B", 1, "z"),
    "6b": onward("A", 3, "x") + onward("B", 3, "z"),
    "7": onward("A", 2, "x") + onward("B", 2, "z"),
}
FIRST = {}
for _name, _moves in ROUNDS.items():
    FIRST[_name] = sum(len(ROUNDS[n]) for n in FIRST)
N_Q = sum(len(m) for m in ROUNDS.values())
PARTS = 4


def kernel(feat, direction, residual, noise, image, coef,
           xq, xp, acc, hq, hp, back, mine, one, two,
           q_send, q_recv, p_send, p_recv, b_send, b_recv, s_send, s_recv):
    me = lax.axis_index("blk")
    core = lax.rem(me, 2)
    y = lax.rem(me // 2, 4)
    x = lax.rem(me // 8, 4)
    z = me // 32

    def dev(dz, dx, dy, dc):
        nz, nx, ny = lax.rem(z + dz, 4), lax.rem(x + dx, 4), lax.rem(y + dy, 4)
        nc = 1 - core if dc else core
        return (((nz * 4 + nx) * 4 + ny) * 2 + nc,)

    def remote(src, dst, send, recv, to):
        return pltpu.make_async_remote_copy(
            src_ref=src, dst_ref=dst, send_sem=send, recv_sem=recv, device_id=to, device_id_type=MESH
        )

    def q_copies(name):
        out = []
        for at, (half, oz, ox, axis, sign, piece) in enumerate(ROUNDS[name]):
            dz, dx = (sign, 0) if axis == "z" else (0, sign)
            src = xq.at[SLOT[half, oz, ox]]
            dst = xq.at[SLOT[half, (oz - dz) % 4, (ox - dx) % 4]]
            if piece is not None:
                rows = pl.ds(piece * (ROWS // 2), ROWS // 2)
                src, dst = src.at[rows], dst.at[rows]
            k = FIRST[name] + at
            out.append(remote(src, dst, q_send.at[k], q_recv.at[k], dev(dz % 4, dx % 4, 0, 0)))
        return out

    def p_copies(name):
        def put(k, src, dst, *to):
            return remote(xp.at[src], xp.at[dst], p_send.at[k], p_recv.at[k], dev(*to))

        pair = pl.ds(2 * core, 2)
        last = pl.ds(12 + 2 * core, 2)
        if name == "own":
            return [put(0, pair, pair, 0, 0, 0, 1)]
        if name in ("first", "second"):
            h = 0 if name == "first" else 1
            at, k = 4 + 4 * h, 1 + 2 * h
            return [put(k, 2 * core + h, at + core, 0, 0, 3, 0), put(k + 1, 2 * core + h, at + 2 + core, 0, 0, 1, 0)]
        if name in ("first over", "second over"):
            h = 0 if name == "first over" else 1
            at, k = 4 + 4 * h, 5 + 2 * h
            return [put(k, at + core, at + core, 0, 0, 0, 1), put(k + 1, at + 2 + core, at + 2 + core, 0, 0, 0, 1)]
        if name == "first on":
            return [put(9, 4 + core, 12 + 2 * core, 0, 0, 3, 0)]
        if name == "second on":
            return [put(10, 10 + core, 13 + 2 * core, 0, 0, 1, 0)]
        return [put(11, last, last, 0, 0, 0, 1)]

    def back_copies(j):
        def put(k, src, dst, *to):
            return remote(acc.at[src], back.at[dst], b_send.at[k], b_recv.at[k], dev(*to))

        out = []
        for dc in range(2):
            target = 1 - core if dc else core
            if j == 0 and dc == 1:
                out.append(put(0, pl.ds(2 * target, 2), pl.ds(0, 2), 0, 0, 0, 1))
            elif j == 3:
                at = 10 + 2 * dc
                out.append(put(1 + dc, pl.ds(12 + 2 * target, 2), pl.ds(at, 2), 0, 0, 2, dc))
            elif j:
                for side, dy in enumerate((1, 3)):
                    at = 2 + 4 * side + 2 * dc + j - 1
                    k = 3 + 4 * (j - 1) + 2 * side + dc
                    out.append(put(k, 4 * j + 2 * side + target, at, 0, 0, dy, dc))
        return out

    def start(copies):
        for copy in copies:
            copy.start()

    def arrived(copies):
        for copy in copies:
            copy.wait_recv()

    group = [(dy, dc) for dy in range(4) for dc in range(2)][1:]
    plane = [(dz, dx) for dz in range(4) for dx in range(4)][1:]

    barrier = pltpu.get_barrier_semaphore()
    near = [(1, 0, 0, 0), (3, 0, 0, 0), (0, 1, 0, 0), (0, 3, 0, 0), (0, 0, 1, 0), (0, 0, 3, 0), (0, 0, 0, 1)]
    for to in near:
        pl.semaphore_signal(barrier, inc=1, device_id=dev(*to), device_id_type=MESH)

    for at in range(2):
        cols = pl.ds(at * HALF, HALF)
        xq[at, 0:HALF, :] = feat[:, cols].T
        xq[at, HALF:ROWS, :] = direction[:, cols].astype(jnp.bfloat16)
        xp[2 * core + at] = feat[:, cols]
    acc[...] = jnp.zeros_like(acc)

    pl.semaphore_wait(barrier, len(near))
    start(q_copies("1"))
    start(p_copies("own") + p_copies("first") + p_copies("second"))
    start(q_copies("2"))

    def task(t, carry):
        far = jnp.maximum(t - NEAR, 0)
        turn = far // FAR
        late = t >= NEAR
        last_j = jnp.where(turn == 0, 3, jnp.where(turn == 3, 0, turn))
        early = t < 8
        early_g = jnp.where(t < 4, t // 2, lax.rem(t, 2))
        early_j = jnp.where(t < 4, lax.rem(t, 2), t // 2)
        g = jnp.where(late, LATE + lax.rem(far, FAR), jnp.where(early, early_g, t // GROUP))
        j = jnp.where(late, last_j, jnp.where(early, early_j, lax.rem(t, GROUP)))

        @pl.when(t == 0)
        def _():
            arrived(p_copies("first"))
            start(p_copies("first over") + p_copies("first on"))
            arrived(q_copies("1"))
            start(q_copies("3") + q_copies("4a") + q_copies("4b"))
            arrived(p_copies("own"))

        @pl.when(t == 1)
        def _():
            arrived(p_copies("first over"))

        @pl.when(t == 2)
        def _():
            arrived(p_copies("second"))
            start(p_copies("second over") + p_copies("second on"))
            arrived(q_copies("2"))
            start(q_copies("4"))

        @pl.when(t == 4)
        def _():
            arrived(p_copies("second over"))
            arrived(q_copies("3"))
            start(q_copies("5"))

        @pl.when(t == 5)
        def _():
            arrived(p_copies("first on") + p_copies("second on"))
            start(p_copies("last over"))

        @pl.when(t == 6)
        def _():
            arrived(p_copies("last over"))

        @pl.when(t == 8)
        def _():
            arrived(q_copies("4a"))
            start(q_copies("6a"))

        @pl.when(t == 11)
        def _():
            arrived(q_copies("4b"))
            start(q_copies("6b"))

        @pl.when(t == 15)
        def _():
            arrived(q_copies("5"))
            start(q_copies("7"))

        @pl.when(t == NEAR)
        def _():
            arrived(q_copies("4"))

        @pl.when(t == NEAR + 1)
        def _():
            arrived(q_copies("6a"))

        @pl.when(t == NEAR + 2)
        def _():
            arrived(q_copies("6b") + q_copies("7"))

        for turn_done, chunk in enumerate((3, 1, 2)):
            @pl.when(t == NEAR + FAR * (turn_done + 1))
            def _(chunk=chunk):
                start(back_copies(chunk))

        slots = pl.ds(g * GROUP, GROUP)
        points = pl.ds(pl.multiple_of(g * GROUP * HALF, GROUP * HALF), GROUP * HALF)

        @pl.when((t == 0) | (t == 1) | (t == 4) | (t == 6))
        def _():
            for c in range(PARTS):
                wide = xp[PARTS * j + c].astype(jnp.float32)
                hp[j, :, c * HALF:(c + 1) * HALF] = (0.5 * LOG2E) * jnp.sum(wide * wide, axis=0, keepdims=True)

        @pl.when((t == 0) | (t == 2) | ((t >= 8) & (j == 0) & (t < NEAR)) | (late & (turn == 0)))
        def _():
            wide = xq[slots, 0:HALF, :].reshape(GROUP * HALF, HALF).astype(jnp.float32)
            hq[points, :] = (0.5 * LOG2E) * jnp.sum(wide * wide, axis=1, keepdims=True)

        rows = xq[slots, 0:HALF, :].reshape(GROUP * HALF, HALF)
        cols = jnp.concatenate([xp[PARTS * j + c] for c in range(PARTS)], axis=1)
        gram = jnp.dot(rows, cols, preferred_element_type=jnp.float32)
        tile = jnp.exp2(gram * LOG2E - hq[points, :] - hp[j]).astype(jnp.bfloat16)
        dirs = jnp.concatenate([xq[g * GROUP + i, HALF:ROWS, :] for i in range(GROUP)], axis=1)
        part = jnp.dot(dirs, tile, preferred_element_type=jnp.float32)
        for c in range(PARTS):
            acc[PARTS * j + c] += part[:, c * HALF:(c + 1) * HALF]
        return carry

    lax.fori_loop(0, NGROUP * GROUP, task, 0)

    backs = [copy for j in (3, 1, 2, 0) for copy in back_copies(j)]
    start(back_copies(0))
    res = residual[...]
    way = direction[...]
    rr = jnp.sum(res * res, axis=1, keepdims=True)
    arrived(backs)
    halves = [acc[2 * core + h] for h in range(2)]
    for k in range(7):
        halves = [halves[h] + back[2 * k + h] for h in range(2)]
    total = jnp.concatenate(halves, axis=1) + noise[0] * way
    image[...] = total
    sums = [rr] + [jnp.sum(v, axis=1, keepdims=True) for v in (way * total, res * total, total * total)]
    lane = lax.broadcasted_iota(jnp.int32, (DIRS, 128), 1)
    packed = jnp.zeros((DIRS, 128), jnp.float32)
    for k, v in enumerate(sums):
        packed = jnp.where(lane == k, v, packed)
    packed = jnp.concatenate([packed, jnp.zeros((128 - DIRS, 128), jnp.float32)], axis=0).T
    mine[0] = packed[0:8]

    firsts = [remote(mine.at[0], one.at[k], s_send.at[k], s_recv.at[k], dev(0, 0, dy, dc))
              for k, (dy, dc) in enumerate(group)]
    start(firsts)
    arrived(firsts)
    so_far = mine[0]
    for k in range(len(group)):
        so_far = so_far + one[k]
    mine[1] = so_far
    n = len(group)
    seconds = [remote(mine.at[1], two.at[k], s_send.at[n + k], s_recv.at[n + k], dev(dz, dx, 0, 0))
               for k, (dz, dx) in enumerate(plane)]
    start(seconds)
    arrived(seconds)
    for k in range(len(plane)):
        so_far = so_far + two[k]
    rr, curv, ri, ii = [so_far[k:k + 1] for k in range(4)]
    rsq = rr + 1e-6
    alpha = rsq / curv
    beta = (rr - alpha * (2.0 * ri - alpha * ii)) / rsq
    coef[...] = jnp.concatenate([alpha, beta, jnp.zeros((6, 128), jnp.float32)], axis=0)

    for name in ROUNDS:
        for copy in q_copies(name):
            copy.wait_send()
    for name in ("own", "first", "second", "first over", "second over", "first on", "second on", "last over"):
        for copy in p_copies(name):
            copy.wait_send()
    for copy in backs + firsts + seconds:
        copy.wait_send()


def shards(features, direction, residual, noise_var):
    vmem = pl.BlockSpec(memory_space=pltpu.VMEM)
    columns, points = direction.shape
    dma = pltpu.SemaphoreType.DMA
    image, coef = pl.pallas_call(
        kernel,
        out_shape=(
            jax.ShapeDtypeStruct((columns, points), jnp.float32),
            jax.ShapeDtypeStruct((8, 128), jnp.float32),
        ),
        in_specs=[vmem, vmem, vmem, pl.BlockSpec(memory_space=pltpu.SMEM)],
        out_specs=(vmem, vmem),
        scratch_shapes=[
            pltpu.VMEM((NGROUP * GROUP, ROWS, HALF), jnp.bfloat16),
            pltpu.VMEM((4 * PARTS, 256, HALF), jnp.bfloat16),
            pltpu.VMEM((4 * PARTS, DIRS, HALF), jnp.float32),
            pltpu.VMEM((NGROUP * GROUP * HALF, 1), jnp.float32),
            pltpu.VMEM((4, 1, PARTS * HALF), jnp.float32),
            pltpu.VMEM((14, DIRS, HALF), jnp.float32),
            pltpu.VMEM((2, 8, 128), jnp.float32),
            pltpu.VMEM((7, 8, 128), jnp.float32),
            pltpu.VMEM((15, 8, 128), jnp.float32),
            dma((N_Q,)), dma((N_Q,)), dma((12,)), dma((12,)), dma((11,)), dma((11,)), dma((22,)), dma((22,)),
        ],
        compiler_params=pltpu.CompilerParams(
            collective_id=0, has_side_effects=True, vmem_limit_bytes=56 * 2**20
        ),
    )(features, direction, residual, noise_var)
    alpha, beta = coef[0, :columns, None], coef[1, :columns, None]
    fresh = residual - alpha * image
    return fresh, fresh + beta * direction


def solution(mesh):
    return jax.shard_map(
        shards,
        mesh=mesh,
        in_specs=(P(None, "blk"), P(None, "blk"), P(None, "blk"), P()),
        out_specs=(P(None, "blk"), P(None, "blk")),
        check_vma=False,
    )
```

```python
import jax
import jax.numpy as jnp
from jax import lax
from jax.experimental import pallas as pl
from jax.experimental.pallas import tpu as pltpu
from jax.sharding import PartitionSpec as P

LOG2E = 1.4426950408889634
MESH = pl.DeviceIdType.MESH
HALF = 256
DIRS = 64
ROWS = HALF + DIRS
GROUP = 4
NGROUP = 8
LATE = 5
NEAR = LATE * GROUP
FAR = NGROUP - LATE

ORDER = (
    ("A", 0, 0), ("B", 0, 0), ("A", 1, 0), ("B", 0, 1),
    ("A", 3, 0), ("B", 0, 3), ("B", 1, 0), ("A", 0, 1),
    ("B", 3, 0), ("A", 0, 3), ("A", 2, 0), ("B", 0, 2),
    ("A", 1, 1), ("A", 1, 3), ("B", 1, 1), ("B", 3, 1),
    ("A", 3, 1), ("A", 3, 3), ("B", 1, 3), ("B", 3, 3),
    ("B", 2, 0), ("A", 0, 2), ("A", 2, 1), ("B", 1, 2),
    ("A", 2, 3), ("B", 3, 2), ("A", 1, 2), ("B", 2, 1),
    ("A", 3, 2), ("B", 2, 3), ("A", 2, 2), ("B", 2, 2),
)
SLOT = {key: at for at, key in enumerate(ORDER)}


def both(half, oz, ox, axis):
    return [(half, oz, ox, axis, -1, None), (half, oz, ox, axis, 1, None)]


def onward(half, other, axis):
    ends = ((1, other), (3, other)) if axis == "z" else ((other, 1), (other, 3))
    return [(half, *ends[0], axis, -1, 0), (half, *ends[1], axis, 1, 1)]


ROUNDS = {
    "1": both("A", 0, 0, "z") + both("B", 0, 0, "x"),
    "2": both("B", 0, 0, "z") + both("A", 0, 0, "x"),
    "3": onward("A", 0, "z") + onward("B", 0, "x"),
    "4a": both("A", 1, 0, "x") + both("B", 0, 1, "z"),
    "4b": both("A", 3, 0, "x") + both("B", 0, 3, "z"),
    "4": onward("B", 0, "z") + onward("A", 0, "x"),
    "5": both("A", 2, 0, "x") + both("B", 0, 2, "z"),
    "6a": onward("A", 1, "x") + onward("B", 1, "z"),
    "6b": onward("A", 3, "x") + onward("B", 3, "z"),
    "7": onward("A", 2, "x") + onward("B", 2, "z"),
}
FIRST = {}
for _name, _moves in ROUNDS.items():
    FIRST[_name] = sum(len(ROUNDS[n]) for n in FIRST)
N_Q = sum(len(m) for m in ROUNDS.values())
PARTS = 4


def kernel(feat, direction, residual, noise, image, coef,
           xq, xp, acc, hq, hp, back, mine, one, two,
           q_send, q_recv, p_send, p_recv, b_send, b_recv, s_send, s_recv):
    me = lax.axis_index("blk")
    core = lax.rem(me, 2)
    y = lax.rem(me // 2, 4)
    x = lax.rem(me // 8, 4)
    z = me // 32

    def dev(dz, dx, dy, dc):
        nz, nx, ny = lax.rem(z + dz, 4), lax.rem(x + dx, 4), lax.rem(y + dy, 4)
        nc = 1 - core if dc else core
        return (((nz * 4 + nx) * 4 + ny) * 2 + nc,)

    def remote(src, dst, send, recv, to):
        return pltpu.make_async_remote_copy(
            src_ref=src, dst_ref=dst, send_sem=send, recv_sem=recv, device_id=to, device_id_type=MESH
        )

    def q_copies(name):
        out = []
        for at, (half, oz, ox, axis, sign, piece) in enumerate(ROUNDS[name]):
            dz, dx = (sign, 0) if axis == "z" else (0, sign)
            src = xq.at[SLOT[half, oz, ox]]
            dst = xq.at[SLOT[half, (oz - dz) % 4, (ox - dx) % 4]]
            if piece is not None:
                rows = pl.ds(piece * (ROWS // 2), ROWS // 2)
                src, dst = src.at[rows], dst.at[rows]
            k = FIRST[name] + at
            out.append(remote(src, dst, q_send.at[k], q_recv.at[k], dev(dz % 4, dx % 4, 0, 0)))
        return out

    def p_copies(name):
        def put(k, src, dst, *to):
            return remote(xp.at[src], xp.at[dst], p_send.at[k], p_recv.at[k], dev(*to))

        pair = pl.ds(2 * core, 2)
        last = pl.ds(12 + 2 * core, 2)
        if name == "own":
            return [put(0, pair, pair, 0, 0, 0, 1)]
        if name in ("first", "second"):
            h = 0 if name == "first" else 1
            at, k = 4 + 4 * h, 1 + 2 * h
            return [put(k, 2 * core + h, at + core, 0, 0, 3, 0), put(k + 1, 2 * core + h, at + 2 + core, 0, 0, 1, 0)]
        if name in ("first over", "second over"):
            h = 0 if name == "first over" else 1
            at, k = 4 + 4 * h, 5 + 2 * h
            return [put(k, at + core, at + core, 0, 0, 0, 1), put(k + 1, at + 2 + core, at + 2 + core, 0, 0, 0, 1)]
        if name == "first on":
            return [put(9, 4 + core, 12 + 2 * core, 0, 0, 3, 0)]
        if name == "second on":
            return [put(10, 10 + core, 13 + 2 * core, 0, 0, 1, 0)]
        return [put(11, last, last, 0, 0, 0, 1)]

    def back_copies(j):
        def put(k, src, dst, *to):
            return remote(acc.at[src], back.at[dst], b_send.at[k], b_recv.at[k], dev(*to))

        out = []
        for dc in range(2):
            target = 1 - core if dc else core
            if j == 0 and dc == 1:
                out.append(put(0, pl.ds(2 * target, 2), pl.ds(0, 2), 0, 0, 0, 1))
            elif j == 3:
                at = 10 + 2 * dc
                out.append(put(1 + dc, pl.ds(12 + 2 * target, 2), pl.ds(at, 2), 0, 0, 2, dc))
            elif j:
                for side, dy in enumerate((1, 3)):
                    at = 2 + 4 * side + 2 * dc + j - 1
                    k = 3 + 4 * (j - 1) + 2 * side + dc
                    out.append(put(k, 4 * j + 2 * side + target, at, 0, 0, dy, dc))
        return out

    def start(copies):
        for copy in copies:
            copy.start()

    def arrived(copies):
        for copy in copies:
            copy.wait_recv()

    group = [(dy, dc) for dy in range(4) for dc in range(2)][1:]
    plane = [(dz, dx) for dz in range(4) for dx in range(4)][1:]

    barrier = pltpu.get_barrier_semaphore()
    near = [(1, 0, 0, 0), (3, 0, 0, 0), (0, 1, 0, 0), (0, 3, 0, 0), (0, 0, 1, 0), (0, 0, 3, 0), (0, 0, 0, 1)]
    for to in near:
        pl.semaphore_signal(barrier, inc=1, device_id=dev(*to), device_id_type=MESH)

    for at in range(2):
        cols = pl.ds(at * HALF, HALF)
        xq[at, 0:HALF, :] = feat[:, cols].T
        xq[at, HALF:ROWS, :] = direction[:, cols].astype(jnp.bfloat16)
        xp[2 * core + at] = feat[:, cols]
    acc[...] = jnp.zeros_like(acc)

    pl.semaphore_wait(barrier, len(near))
    start(q_copies("1"))
    start(p_copies("own") + p_copies("first") + p_copies("second"))
    start(q_copies("2"))

    def task(t, carry):
        far = max(t - NEAR, 0)
        turn = far // FAR
        late = t >= NEAR
        if late:
            g, j = LATE + far % FAR, (3, 1, 2, 0)[turn]
        elif t < 8:
            g, j = (0, 0, 1, 1, 0, 1, 0, 1)[t], (0, 1, 0, 1, 2, 2, 3, 3)[t]
        else:
            g, j = t // GROUP, t % GROUP

        if t == 0:
            arrived(p_copies("first"))
            start(p_copies("first over") + p_copies("first on"))
            arrived(q_copies("1"))
            start(q_copies("3") + q_copies("4a") + q_copies("4b"))
            arrived(p_copies("own"))

        if t == 1:
            arrived(p_copies("first over"))

        if t == 2:
            arrived(p_copies("second"))
            start(p_copies("second over") + p_copies("second on"))
            arrived(q_copies("2"))
            start(q_copies("4"))

        if t == 4:
            arrived(p_copies("second over"))
            arrived(q_copies("3"))
            start(q_copies("5"))

        if t == 5:
            arrived(p_copies("first on") + p_copies("second on"))
            start(p_copies("last over"))

        if t == 6:
            arrived(p_copies("last over"))

        if t == 8:
            arrived(q_copies("4a"))
            start(q_copies("6a"))

        if t == 11:
            arrived(q_copies("4b"))
            start(q_copies("6b"))

        if t == 15:
            arrived(q_copies("5"))
            start(q_copies("7"))

        if t == NEAR:
            arrived(q_copies("4"))

        if t == NEAR + 1:
            arrived(q_copies("6a"))

        if t == NEAR + 2:
            arrived(q_copies("6b") + q_copies("7"))

        for turn_done, chunk in enumerate((3, 1, 2)):
            if t == NEAR + FAR * (turn_done + 1):
                start(back_copies(chunk))

        slots = pl.ds(g * GROUP, GROUP)
        points = pl.ds(g * GROUP * HALF, GROUP * HALF)

        if (t == 0) or (t == 1) or (t == 4) or (t == 6):
            for c in range(PARTS):
                wide = xp[PARTS * j + c].astype(jnp.float32)
                hp[j, :, c * HALF:(c + 1) * HALF] = (0.5 * LOG2E) * jnp.sum(wide * wide, axis=0, keepdims=True)

        if (t == 0) or (t == 2) or ((t >= 8) and (j == 0) and (t < NEAR)) or (late and (turn == 0)):
            wide = xq[slots, 0:HALF, :].reshape(GROUP * HALF, HALF).astype(jnp.float32)
            hq[points, :] = (0.5 * LOG2E) * jnp.sum(wide * wide, axis=1, keepdims=True)

        rows = xq[slots, 0:HALF, :].reshape(GROUP * HALF, HALF)
        cols = jnp.concatenate([xp[PARTS * j + c] for c in range(PARTS)], axis=1)
        gram = jnp.dot(rows, cols, preferred_element_type=jnp.float32)
        tile = jnp.exp2(gram * LOG2E - hq[points, :] - hp[j]).astype(jnp.bfloat16)
        dirs = jnp.concatenate([xq[g * GROUP + i, HALF:ROWS, :] for i in range(GROUP)], axis=1)
        part = jnp.dot(dirs, tile, preferred_element_type=jnp.float32)
        for c in range(PARTS):
            acc[PARTS * j + c] += part[:, c * HALF:(c + 1) * HALF]
        return carry

    for t in range(NGROUP * GROUP):
        task(t, 0)

    backs = [copy for j in (3, 1, 2, 0) for copy in back_copies(j)]
    start(back_copies(0))
    res = residual[...]
    way = direction[...]
    rr = jnp.sum(res * res, axis=1, keepdims=True)
    arrived(backs)
    halves = [acc[2 * core + h] for h in range(2)]
    for k in range(7):
        halves = [halves[h] + back[2 * k + h] for h in range(2)]
    total = jnp.concatenate(halves, axis=1) + noise[0] * way
    image[...] = total
    sums = [rr] + [jnp.sum(v, axis=1, keepdims=True) for v in (way * total, res * total, total * total)]
    lane = lax.broadcasted_iota(jnp.int32, (DIRS, 128), 1)
    upper = jnp.where(lane == 0, sums[0], jnp.where(lane == 1, sums[2], 0.0))
    lower = jnp.where(lane == 0, sums[1], jnp.where(lane == 1, sums[3], 0.0))
    mine[0] = jnp.concatenate([upper, lower], axis=0).T[0:8]
    top = pl.ds(0, 2)

    firsts = [remote(mine.at[0, top], one.at[k, top], s_send.at[k], s_recv.at[k], dev(0, 0, dy, dc))
              for k, (dy, dc) in enumerate(group)]
    start(firsts)
    arrived(firsts)
    so_far = mine[0, top]
    for k in range(len(group)):
        so_far = so_far + one[k, top]
    mine[1, top] = so_far
    n = len(group)
    seconds = [remote(mine.at[1, top], two.at[k, top], s_send.at[n + k], s_recv.at[n + k], dev(dz, dx, 0, 0))
               for k, (dz, dx) in enumerate(plane)]
    start(seconds)
    arrived(seconds)
    for k in range(len(plane)):
        so_far = so_far + two[k, top]
    columns = jnp.concatenate([so_far, jnp.zeros((126, 128), jnp.float32)], axis=0).T
    rr, curv = columns[0:DIRS, 0:1], columns[DIRS:, 0:1]
    ri, ii = columns[0:DIRS, 1:2], columns[DIRS:, 1:2]
    rsq = rr + 1e-6
    alpha = rsq / curv
    beta = (rr - alpha * (2.0 * ri - alpha * ii)) / rsq
    coef[...] = jnp.where(lane == 0, alpha, beta)

    for name in ROUNDS:
        for copy in q_copies(name):
            copy.wait_send()
    for name in ("own", "first", "second", "first over", "second over", "first on", "second on", "last over"):
        for copy in p_copies(name):
            copy.wait_send()
    for copy in backs + firsts + seconds:
        copy.wait_send()


def shards(features, direction, residual, noise_var):
    vmem = pl.BlockSpec(memory_space=pltpu.VMEM)
    columns, points = direction.shape
    dma = pltpu.SemaphoreType.DMA
    image, coef = pl.pallas_call(
        kernel,
        out_shape=(
            jax.ShapeDtypeStruct((columns, points), jnp.float32),
            jax.ShapeDtypeStruct((columns, 128), jnp.float32),
        ),
        in_specs=[vmem, vmem, vmem, pl.BlockSpec(memory_space=pltpu.SMEM)],
        out_specs=(vmem, vmem),
        scratch_shapes=[
            pltpu.VMEM((NGROUP * GROUP, ROWS, HALF), jnp.bfloat16),
            pltpu.VMEM((4 * PARTS, 256, HALF), jnp.bfloat16),
            pltpu.VMEM((4 * PARTS, DIRS, HALF), jnp.float32),
            pltpu.VMEM((NGROUP * GROUP * HALF, 1), jnp.float32),
            pltpu.VMEM((4, 1, PARTS * HALF), jnp.float32),
            pltpu.VMEM((14, DIRS, HALF), jnp.float32),
            pltpu.VMEM((2, 8, 128), jnp.float32),
            pltpu.VMEM((7, 8, 128), jnp.float32),
            pltpu.VMEM((15, 8, 128), jnp.float32),
            dma((N_Q,)), dma((N_Q,)), dma((12,)), dma((12,)), dma((11,)), dma((11,)), dma((22,)), dma((22,)),
        ],
        compiler_params=pltpu.CompilerParams(
            collective_id=0, has_side_effects=True, vmem_limit_bytes=56 * 2**20
        ),
    )(features, direction, residual, noise_var)
    alpha, beta = coef[:, 0:1], coef[:, 1:2]
    fresh = residual - alpha * image
    return fresh, fresh + beta * direction


def solution(mesh):
    return jax.shard_map(
        shards,
        mesh=mesh,
        in_specs=(P(None, "blk"), P(None, "blk"), P(None, "blk"), P()),
        out_specs=(P(None, "blk"), P(None, "blk")),
        check_vma=False,
    )
```

```python
import jax
import jax.numpy as jnp
from jax import lax
from jax.experimental import pallas as pl
from jax.experimental.pallas import tpu as pltpu
from jax.sharding import PartitionSpec as P

LOG2E = 1.4426950408889634
MESH = pl.DeviceIdType.MESH
HALF = 256
DIRS = 64
ROWS = HALF + DIRS
N_HALF = 32

ORDER = (
    ("A", 0, 0), ("B", 0, 0),
    ("A", 1, 0), ("B", 0, 1), ("A", 3, 0), ("B", 0, 3),
    ("B", 1, 0), ("A", 0, 1), ("B", 3, 0), ("A", 0, 3),
    ("A", 1, 1), ("A", 1, 3), ("B", 1, 1), ("B", 3, 1),
    ("A", 3, 1), ("A", 3, 3), ("B", 1, 3), ("B", 3, 3),
    ("A", 2, 0), ("B", 0, 2), ("B", 2, 0), ("A", 0, 2),
    ("A", 2, 1), ("B", 1, 2), ("A", 2, 3), ("B", 3, 2),
    ("A", 1, 2), ("B", 2, 1), ("A", 3, 2), ("B", 2, 3), ("A", 2, 2), ("B", 2, 2),
)
OWN, G1, G01, G2, G3, G4, G5, G6, G7 = (
    (0, 2), (2, 6), (0, 6), (6, 10), (10, 14), (14, 18), (18, 22), (22, 26), (26, 32)
)
SLOT = {key: at for at, key in enumerate(ORDER)}


def both(half, oz, ox, axis):
    return [(half, oz, ox, axis, -1, None), (half, oz, ox, axis, 1, None)]


def onward(half, other, axis):
    ends = ((1, other), (3, other)) if axis == "z" else ((other, 1), (other, 3))
    return [(half, *ends[0], axis, -1, 0), (half, *ends[1], axis, 1, 1)]


ROUNDS = {
    "1": both("A", 0, 0, "z") + both("B", 0, 0, "x"),
    "2": both("B", 0, 0, "z") + both("A", 0, 0, "x"),
    "3": onward("A", 0, "z") + onward("B", 0, "x"),
    "4a": both("A", 1, 0, "x") + both("B", 0, 1, "z"),
    "4b": both("A", 3, 0, "x") + both("B", 0, 3, "z"),
    "4": onward("B", 0, "z") + onward("A", 0, "x"),
    "5": both("A", 2, 0, "x") + both("B", 0, 2, "z"),
    "6a": onward("A", 1, "x") + onward("B", 1, "z"),
    "6b": onward("A", 3, "x") + onward("B", 3, "z"),
    "7": onward("A", 2, "x") + onward("B", 2, "z"),
}
FIRST = {}
for _name, _moves in ROUNDS.items():
    FIRST[_name] = sum(len(ROUNDS[n]) for n in FIRST)
N_Q = sum(len(m) for m in ROUNDS.values())
PARTS = 4


def kernel(feat_in, direction_in, residual_in, noise, step, turn,
           feat, direction, residual, load_sem, xq, xp, acc, hq, hp, back, far_out, far_in, mine, one, two,
           q_send, q_recv, p_send, p_recv, b_send, b_recv, s_send, s_recv):
    me = lax.axis_index("blk")
    core = lax.rem(me, 2)
    y = lax.rem(me // 2, 4)
    x = lax.rem(me // 8, 4)
    z = me // 32

    def dev(dz, dx, dy, dc):
        nz, nx, ny = lax.rem(z + dz, 4), lax.rem(x + dx, 4), lax.rem(y + dy, 4)
        nc = 1 - core if dc else core
        return (((nz * 4 + nx) * 4 + ny) * 2 + nc,)

    def remote(src, dst, send, recv, to):
        return pltpu.make_async_remote_copy(
            src_ref=src, dst_ref=dst, send_sem=send, recv_sem=recv, device_id=to, device_id_type=MESH
        )

    def q_copies(name):
        out = []
        for at, (half, oz, ox, axis, sign, piece) in enumerate(ROUNDS[name]):
            dz, dx = (sign, 0) if axis == "z" else (0, sign)
            src = xq.at[SLOT[half, oz, ox]]
            dst = xq.at[SLOT[half, (oz - dz) % 4, (ox - dx) % 4]]
            if piece is not None:
                rows = pl.ds(piece * (ROWS // 2), ROWS // 2)
                src, dst = src.at[rows], dst.at[rows]
            k = FIRST[name] + at
            out.append(remote(src, dst, q_send.at[k], q_recv.at[k], dev(dz % 4, dx % 4, 0, 0)))
        return out

    def p_copies(name):
        def put(k, src, dst, *to):
            return remote(xp.at[src], xp.at[dst], p_send.at[k], p_recv.at[k], dev(*to))

        pair = pl.ds(2 * core, 2)
        last = pl.ds(12 + 2 * core, 2)
        if name == "own":
            return [put(0, pair, pair, 0, 0, 0, 1)]
        if name in ("first", "second"):
            h = 0 if name == "first" else 1
            at, k = 4 + 4 * h, 1 + 2 * h
            return [put(k, 2 * core + h, at + core, 0, 0, 3, 0), put(k + 1, 2 * core + h, at + 2 + core, 0, 0, 1, 0)]
        if name in ("first over", "second over"):
            h = 0 if name == "first over" else 1
            at, k = 4 + 4 * h, 5 + 2 * h
            return [put(k, at + core, at + core, 0, 0, 0, 1), put(k + 1, at + 2 + core, at + 2 + core, 0, 0, 0, 1)]
        if name == "first on":
            return [put(9, 4 + core, 12 + 2 * core, 0, 0, 3, 0)]
        if name == "second on":
            return [put(10, 10 + core, 13 + 2 * core, 0, 0, 1, 0)]
        return [put(11, last, last, 0, 0, 0, 1)]

    def back_copies(j):
        def put(k, src, dst, *to):
            return remote(src, dst, b_send.at[k], b_recv.at[k], dev(*to))

        out = []
        for dc in range(2):
            target = 1 - core if dc else core
            if j == 0 and dc == 1:
                out.append(put(0, acc.at[pl.ds(2 * target, 2)], back.at[pl.ds(0, 2)], 0, 0, 0, 1))
            elif j == 3:
                out.append(put(1 + dc, far_out.at[pl.ds(2 * target, 2)], far_in.at[pl.ds(2 * dc, 2)], 0, 0, 2, dc))
            elif j:
                for side, dy in enumerate((1, 3)):
                    k = 3 + 4 * (j - 1) + 2 * side + dc
                    if j == 1:
                        src, dst = acc.at[4 + 2 * side + target], back.at[2 + 2 * side + dc]
                    else:
                        src, dst = far_out.at[4 + 2 * side + target], far_in.at[4 + 2 * side + dc]
                    out.append(put(k, src, dst, 0, 0, dy, dc))
        return out

    def start(copies):
        for copy in copies:
            copy.start()

    def arrived(copies):
        for copy in copies:
            copy.wait_recv()

    group = [(dy, dc) for dy in range(4) for dc in range(2)][1:]
    plane = [(dz, dx) for dz in range(4) for dx in range(4)][1:]

    barrier = pltpu.get_barrier_semaphore()
    near = [(1, 0, 0, 0), (3, 0, 0, 0), (0, 1, 0, 0), (0, 3, 0, 0), (0, 0, 1, 0), (0, 0, 3, 0), (0, 0, 0, 1)]
    for to in near:
        pl.semaphore_signal(barrier, inc=1, device_id=dev(*to), device_id_type=MESH)

    loads = [
        pltpu.make_async_copy(src, dst, load_sem.at[k])
        for k, (src, dst) in enumerate(((feat_in, feat), (direction_in, direction), (residual_in, residual)))
    ]
    start(loads)
    loads[0].wait()
    loads[1].wait()
    for at in range(2):
        cols = pl.ds(at * HALF, HALF)
        xq[at, 0:HALF, :] = feat[:, cols].T
        xq[at, HALF:ROWS, :] = direction[:, cols].astype(jnp.bfloat16)
        xp[2 * core + at] = feat[:, cols]

    pl.semaphore_wait(barrier, len(near))
    start(q_copies("1"))
    start(p_copies("own") + p_copies("first") + p_copies("second"))
    start(q_copies("2"))

    def point_norms(first, end):
        for at in range(first, end):
            wide = xq[at, 0:HALF, :].astype(jnp.float32)
            hq[at * HALF:(at + 1) * HALF, :] = (0.5 * LOG2E) * jnp.sum(wide * wide, axis=1, keepdims=True)

    def part_norms(*parts):
        for at in parts:
            wide = xp[at].astype(jnp.float32)
            hp[at] = (0.5 * LOG2E) * jnp.sum(wide * wide, axis=0, keepdims=True)

    def tile(group, parts, new=False):
        first, end = group
        rows = xq[first:end, 0:HALF, :].reshape((end - first) * HALF, HALF)
        cols = jnp.concatenate([xp[at] for at in parts], axis=1)
        shift = jnp.concatenate([hp[at] for at in parts], axis=1)
        gram = jnp.dot(rows, cols, preferred_element_type=jnp.float32)
        values = jnp.exp2(gram * LOG2E - hq[first * HALF:end * HALF, :] - shift).astype(jnp.bfloat16)
        dirs = jnp.concatenate([xq[at, HALF:ROWS, :] for at in range(first, end)], axis=1)
        total = jnp.dot(dirs, values, preferred_element_type=jnp.float32)
        for k, at in enumerate(parts):
            piece = total[:, k * HALF:(k + 1) * HALF]
            acc[at] = piece if new else acc[at] + piece

    chunk = [range(4 * j, 4 * j + 4) for j in range(4)]
    theirs = (2 * (1 - core), 2 * (1 - core) + 1)
    ours = (2 * core, 2 * core + 1)

    point_norms(*OWN)
    arrived(p_copies("own"))
    part_norms(*chunk[0])
    tile(OWN, chunk[0], new=True)
    loads[2].wait()
    rr = jnp.sum(residual[...] * residual[...], axis=1, keepdims=True)
    arrived(p_copies("first"))
    start(p_copies("first over") + p_copies("first on"))
    arrived(q_copies("1"))
    start(q_copies("3") + q_copies("4a") + q_copies("4b"))
    point_norms(*G1)
    tile(G1, chunk[0])
    arrived(p_copies("first over"))
    part_norms(*chunk[1])
    tile(G01, chunk[1], new=True)
    arrived(p_copies("second"))
    start(p_copies("second over") + p_copies("second on"))
    arrived(q_copies("2"))
    point_norms(*G2)
    tile(G2, chunk[0])
    tile(G2, chunk[1])
    arrived(q_copies("3"))
    start(q_copies("5") + q_copies("4"))
    arrived(p_copies("second over"))
    part_norms(*chunk[2])
    tile(G01, chunk[2], new=True)
    arrived(p_copies("first on") + p_copies("second on"))
    start(p_copies("last over"))
    tile(G2, chunk[2])
    arrived(p_copies("last over"))
    part_norms(*chunk[3])
    tile(G01, chunk[3], new=True)
    arrived(q_copies("4a"))
    start(q_copies("6a"))
    tile(G2, chunk[3])
    point_norms(*G3)
    tile(G3, chunk[0])
    tile(G3, chunk[1])
    tile(G3, chunk[2])
    arrived(q_copies("4b"))
    start(q_copies("6b"))
    tile(G3, chunk[3])
    point_norms(*G4)
    tile(G4, chunk[0])
    arrived(q_copies("5"))
    start(q_copies("7"))
    tile(G4, chunk[1])
    tile(G4, chunk[2])
    tile(G4, chunk[3])
    arrived(q_copies("4"))
    point_norms(*G5)
    point_norms(*G6)
    tile(G5, chunk[3])
    tile(G6, chunk[3])
    tile(G5, chunk[1])
    tile(G6, chunk[1])
    arrived(q_copies("6a") + q_copies("6b") + q_copies("7"))
    point_norms(*G7)
    tile(G7, chunk[3])
    for at in range(4):
        far_out[at] = acc[12 + at].astype(jnp.bfloat16)
    start(back_copies(3))
    tile(G7, chunk[1])
    start(back_copies(1))
    for some in (G5, G6, G7):
        tile(some, chunk[2])
    for at in range(4):
        far_out[4 + at] = acc[8 + at].astype(jnp.bfloat16)
    start(back_copies(2))
    for some in (G5, G6, G7):
        tile(some, theirs)
    start(back_copies(0))
    for some in (G5, G6, G7):
        tile(some, ours)

    backs = [copy for j in (3, 1, 2, 0) for copy in back_copies(j)]
    res, way = residual[...], direction[...]
    arrived(backs)
    halves = [acc[2 * core + h] for h in range(2)]
    halves = [halves[h] + back[h] + far_in[h].astype(jnp.float32) + far_in[2 + h].astype(jnp.float32) for h in range(2)]
    for k in range(4):
        halves = [halves[0] + back[2 + k], halves[1] + far_in[4 + k].astype(jnp.float32)]
    total = jnp.concatenate(halves, axis=1) + noise[0] * way
    sums = [rr] + [jnp.sum(v, axis=1, keepdims=True) for v in (way * total, res * total, total * total)]
    lane = lax.broadcasted_iota(jnp.int32, (DIRS, 128), 1)
    upper = jnp.where(lane == 0, sums[0], jnp.where(lane == 1, sums[2], 0.0))
    lower = jnp.where(lane == 0, sums[1], jnp.where(lane == 1, sums[3], 0.0))
    mine[0] = jnp.concatenate([upper, lower], axis=0).T[0:8]
    top = pl.ds(0, 2)

    firsts = [remote(mine.at[0, top], one.at[k, top], s_send.at[k], s_recv.at[k], dev(0, 0, dy, dc))
              for k, (dy, dc) in enumerate(group)]
    start(firsts)
    for name in ROUNDS:
        for copy in q_copies(name):
            copy.wait_send()
    for name in ("own", "first", "second", "first over", "second over", "first on", "second on", "last over"):
        for copy in p_copies(name):
            copy.wait_send()
    for copy in backs:
        copy.wait_send()
    arrived(firsts)
    so_far = mine[0, top]
    for k in range(len(group)):
        so_far = so_far + one[k, top]
    mine[1, top] = so_far
    n = len(group)
    seconds = [remote(mine.at[1, top], two.at[k, top], s_send.at[n + k], s_recv.at[n + k], dev(dz, dx, 0, 0))
               for k, (dz, dx) in enumerate(plane)]
    start(seconds)
    arrived(seconds)
    for k in range(len(plane)):
        so_far = so_far + two[k, top]
    columns = jnp.concatenate([so_far, jnp.zeros((126, 128), jnp.float32)], axis=0).T
    rr, curv = columns[0:DIRS, 0:1], columns[DIRS:, 0:1]
    ri, ii = columns[0:DIRS, 1:2], columns[DIRS:, 1:2]
    rsq = rr + 1e-6
    alpha = rsq / curv
    beta = (rr - alpha * (2.0 * ri - alpha * ii)) / rsq
    step[...] = alpha * total
    turn[...] = beta * direction[...]

    for copy in firsts + seconds:
        copy.wait_send()


def shards(features, direction, residual, noise_var):
    vmem = pl.BlockSpec(memory_space=pltpu.VMEM)
    hbm = pl.BlockSpec(memory_space=pl.ANY)
    columns, points = direction.shape
    dma = pltpu.SemaphoreType.DMA
    step, turn = pl.pallas_call(
        kernel,
        out_shape=(
            jax.ShapeDtypeStruct((columns, points), jnp.float32),
            jax.ShapeDtypeStruct((columns, points), jnp.float32),
        ),
        in_specs=[hbm, hbm, hbm, pl.BlockSpec(memory_space=pltpu.SMEM)],
        out_specs=(vmem, vmem),
        scratch_shapes=[
            pltpu.VMEM(features.shape, jnp.bfloat16),
            pltpu.VMEM(direction.shape, jnp.float32),
            pltpu.VMEM(residual.shape, jnp.float32),
            dma((3,)),
            pltpu.VMEM((N_HALF, ROWS, HALF), jnp.bfloat16),
            pltpu.VMEM((4 * PARTS, 256, HALF), jnp.bfloat16),
            pltpu.VMEM((4 * PARTS, DIRS, HALF), jnp.float32),
            pltpu.VMEM((N_HALF * HALF, 1), jnp.float32),
            pltpu.VMEM((4 * PARTS, 1, HALF), jnp.float32),
            pltpu.VMEM((6, DIRS, HALF), jnp.float32),
            pltpu.VMEM((8, DIRS, HALF), jnp.bfloat16),
            pltpu.VMEM((8, DIRS, HALF), jnp.bfloat16),
            pltpu.VMEM((2, 8, 128), jnp.float32),
            pltpu.VMEM((7, 8, 128), jnp.float32),
            pltpu.VMEM((15, 8, 128), jnp.float32),
            dma((N_Q,)), dma((N_Q,)), dma((12,)), dma((12,)), dma((11,)), dma((11,)), dma((22,)), dma((22,)),
        ],
        compiler_params=pltpu.CompilerParams(
            collective_id=0, has_side_effects=True, vmem_limit_bytes=56 * 2**20
        ),
    )(features, direction, residual, noise_var)
    fresh = residual - step
    return fresh, fresh + turn


def solution(mesh):
    return jax.shard_map(
        shards,
        mesh=mesh,
        in_specs=(P(None, "blk"), P(None, "blk"), P(None, "blk"), P()),
        out_specs=(P(None, "blk"), P(None, "blk")),
        check_vma=False,
    )
```
